32 devices in a mesh: groups: 2 (over y), expert: 16 (over z, x, core).
Axes of the slice: x: 2, y: 2, z: 4, core: 2. Of those that a mesh axis runs over, the one named last changes fastest.
Arguments:
- tokens: bfloat16 [2048, 2048], P(('groups', 'expert')), parts along dimension 0, may hold values from -6 to 6
- expert_ids: int32 [2048, 8], P(('groups', 'expert')), parts along dimension 0, may hold values from 0 to 15, as said below
- gate_units: int32 [2048, 8], P(('groups', 'expert')), parts along dimension 0, may hold values from 1 to 16
- gate_matrix: bfloat16 [16, 2048, 768], P('expert'), may hold values from -0.125 to 0.125
- up_matrix: bfloat16 [16, 2048, 768], P('expert'), may hold values from -0.125 to 0.125
- down_matrix: bfloat16 [16, 768, 2048], P('expert'), may hold values from -0.21875 to 0.21875
Outputs:
- mixed: bfloat16 [2048, 2048], P(('groups', 'expert')), parts along dimension 0
The draws below stay inside these ranges and needn't reach their ends.
There are 2 independent parts, one for each index of `groups`. The reference program is written for one: setup_inputs(seed, part) draws one part's arguments, and reference() takes and returns one part's arrays. A program takes and returns all parts, laid end to end along the dimension named above; an argument that names none is the same for every part. Nothing has to cross between parts.
Inputs may be any that keep to these rules, and one draw needn't show every extreme that they name: `expert_ids`: each row names 8 different experts. The same 8 experts are named exactly 64 times by the rows of every device; for each of them the expert numbered 16 // 2 higher or lower is named by no row; every other expert is named exactly 64 // 2 times by the rows of every device.
All inputs are finite; a program needn't handle non-finite values.
Results may differ from the reference program's by a relative error of at most 0.0085.
Values may be sent and summed in bfloat16 or wider, within the bound.
No kernel may reach another device: no remote copies, remote signals or barrier semaphores. Data moves between devices by JAX's collectives and lax.ppermute only.
A program may use at most 128 MiB of HBM per device.

```python
import jax
import jax.numpy as jnp
from jax import lax

D = 2048
FF = 768
TOP = 8
HOT = 8
TOK_DEV = 64
EXPERTS = 16
TOKENS = 1024
CAP = 64
N_EXPERT = 16


def draw_expert_ids(key, part):
    key = jax.random.fold_in(key, 7)
    pair_key, flip_key, block_key = jax.random.split(key, 3)
    half_experts = EXPERTS // 2
    pair_bases = jax.random.permutation(pair_key, half_experts)[:HOT]
    flip_bits = jax.random.randint(flip_key, (HOT,), 0, 2)
    busy_ids = pair_bases + flip_bits * half_experts
    empty_ids = pair_bases + (1 - flip_bits) * half_experts
    route_loads = jnp.full((EXPERTS,), CAP // 2, jnp.int32)
    route_loads = route_loads.at[busy_ids].set(CAP).at[empty_ids].set(0)
    block_count = TOKENS // TOK_DEV

    def one_block(block_seed):
        order_key, row_key = jax.random.split(block_seed)
        expert_order = jax.random.permutation(order_key, EXPERTS)
        load_ends = jnp.cumsum(route_loads[expert_order])
        positions = jnp.arange(TOK_DEV * TOP)
        run_index = jnp.sum((load_ends[None, :] <= positions[:, None]).astype(jnp.int32), axis=1)
        sequence = expert_order[run_index]
        id_grid = sequence.reshape(TOP, TOK_DEV).T
        return id_grid[jax.random.permutation(row_key, TOK_DEV)]
    blocks = jax.vmap(one_block)(jax.random.split(block_key, block_count))
    return blocks.reshape(TOKENS, TOP).astype(jnp.int32)


def with_ends(entries, rng, least, largest):
    longest = entries.shape.index(max(entries.shape))
    spots = []
    for shift in (0, 1):
        where = [jax.random.randint(jax.random.fold_in(rng, axis), (), 0, length) for axis, length in enumerate(entries.shape)]
        where[longest] = (where[longest] + shift) % entries.shape[longest]
        spots.append(tuple(where))
    return entries.at[spots[0]].set(least).at[spots[1]].set(largest)


def levels(rng, shape, pieces, low, high):
    level, own = 1.0, jax.random.fold_in(rng, 6)
    for position, parts in pieces:
        steps = jnp.exp(jax.random.uniform(jax.random.fold_in(own, position), (parts,), jnp.float32, low / len(pieces), high / len(pieces)))
        level = level * jnp.repeat(steps, shape[position] // parts).reshape([-1 if axis == position else 1 for axis in range(len(shape))])
    return level


def noise(rng, shape, scale, most, cuts=(), held_as=jnp.bfloat16):
    values = scale * jax.random.normal(rng, shape, jnp.float32)
    if cuts:
        values = values * levels(rng, shape, cuts, -0.22, 0.18)
    return jnp.clip(values, -most, most).astype(held_as)


def setup_inputs(seed: int = 0, part: int = 0) -> dict:
    arg_keys = jax.random.split(jax.random.key(seed), 7)
    part_splits = jax.random.split(jax.random.fold_in(arg_keys[6], part), 7)
    return {
        "tokens": noise(part_splits[0], (TOKENS, D), 1.0, 6.0, ((0, 16),)),
        "expert_ids": draw_expert_ids(jax.random.fold_in(jax.random.fold_in(arg_keys[6], part), 71), part),
        "gate_units": with_ends(jax.random.randint(part_splits[2], (TOKENS, TOP), 1, 17), jax.random.fold_in(part_splits[2], 1), 1, 16).astype(jnp.int32),
        "gate_matrix": noise(arg_keys[3], (EXPERTS, D, FF), D ** -0.5, 0.125, ((0, 16),)),
        "up_matrix": noise(arg_keys[4], (EXPERTS, D, FF), D ** -0.5, 0.125, ((0, 16),)),
        "down_matrix": noise(arg_keys[5], (EXPERTS, FF, D), FF ** -0.5, 0.21875, ((0, 16),)),
    }


def swiglu_rows(rows_in, gate_w, up_w, down_w):
    gate_value = jnp.dot(rows_in, gate_w, preferred_element_type=jnp.float32)
    upward = jnp.dot(rows_in, up_w, preferred_element_type=jnp.float32)
    hidden = (jax.nn.silu(gate_value) * upward).astype(jnp.bfloat16)
    return jnp.dot(hidden, down_w, preferred_element_type=jnp.float32).astype(jnp.bfloat16)


def reference(tokens, expert_ids, gate_units, gate_matrix, up_matrix, down_matrix):
    gate_scale = gate_units.astype(jnp.float32)
    weight = gate_scale / jnp.sum(gate_scale, axis=1, keepdims=True)
    flat_ids = expert_ids.reshape(TOKENS * TOP)
    flat_weight = weight.reshape(TOKENS * TOP)
    limit = N_EXPERT * CAP

    def one_expert(total, inputs):
        expert_index, gate_w, up_w, down_w = inputs
        chosen = flat_ids == expert_index
        picked = jnp.nonzero(chosen, size=limit, fill_value=0)[0].astype(jnp.int32)
        valid = jnp.arange(limit, dtype=jnp.int32) < jnp.sum(chosen.astype(jnp.int32))
        token_index = picked // TOP
        result = swiglu_rows(tokens[token_index], gate_w, up_w, down_w)
        scale_rows = jnp.where(valid, flat_weight[picked], jnp.zeros((), jnp.float32))
        total = total.at[token_index].add(scale_rows[:, None] * result.astype(jnp.float32))
        return total, None

    start_total = jnp.zeros((TOKENS, D), jnp.float32)
    total, unused = lax.scan(one_expert, start_total, (jnp.arange(EXPERTS, dtype=jnp.int32), gate_matrix, up_matrix, down_matrix))
    return total.astype(jnp.bfloat16)
```

```python
import functools

import jax
import jax.numpy as jnp
from jax import lax
from jax.experimental import pallas as pl
from jax.experimental.pallas import tpu as pltpu
from jax.sharding import PartitionSpec as P

LANES = 128
PLANE = 4


def swiglu_rows(rows_in, gate_w, up_w, down_w):
    gate_value = jnp.dot(rows_in, gate_w, preferred_element_type=jnp.float32)
    upward = jnp.dot(rows_in, up_w, preferred_element_type=jnp.float32)
    hidden = (jax.nn.silu(gate_value) * upward).astype(jnp.bfloat16)
    return jnp.dot(hidden, down_w, preferred_element_type=jnp.float32).astype(jnp.bfloat16)


def routed_plan(tokens, expert_ids, gate_units, gate_matrix, up_matrix, down_matrix):
    devices = lax.axis_size("expert")
    tok_rows, top_count = expert_ids.shape
    feature_width = tokens.shape[1]
    route_rows = tok_rows * top_count
    capacity = 2 * route_rows // devices
    flat_ids = expert_ids.reshape(route_rows)
    expert_range = jnp.arange(devices, dtype=jnp.int32)
    onehot = (flat_ids[:, None] == expert_range[None, :]).astype(jnp.int32)
    earlier = jnp.cumsum(onehot, axis=0) - onehot
    position = jnp.sum(earlier * onehot, axis=1)
    routed = jnp.repeat(tokens, top_count, axis=0)
    gate_scale = gate_units.astype(jnp.float32)
    weight = gate_scale / jnp.sum(gate_scale, axis=1, keepdims=True)
    flat_slot = flat_ids * capacity + position
    outgoing = (
        jnp.zeros((devices * capacity, feature_width), jnp.bfloat16).at[flat_slot].set(routed)
    )
    received = lax.all_to_all(
        outgoing.reshape(devices, capacity, feature_width),
        "expert",
        split_axis=0,
        concat_axis=0,
        tiled=True,
    )
    result = swiglu_rows(
        received.reshape(-1, feature_width), gate_matrix[0], up_matrix[0], down_matrix[0]
    )
    back_buffer = lax.all_to_all(
        result.reshape(received.shape), "expert", split_axis=0, concat_axis=0, tiled=True
    )
    returned = back_buffer.reshape(-1, feature_width)[flat_slot]
    expert_out = returned.reshape(tok_rows, top_count, feature_width).astype(jnp.float32)
    mixed = jnp.einsum("tk,tkd->td", weight, expert_out)
    return mixed.astype(jnp.bfloat16)


def expert_kernel(own_ref, *refs):
    blocks, (gate_ref, up_ref, down_ref) = refs[:PLANE], refs[PLANE : PLANE + 3]
    outs = refs[PLANE + 3 : 2 * PLANE + 3]
    rows_ref, total_ref = refs[2 * PLANE + 3 :]
    step, steps = pl.program_id(0), pl.num_programs(0)
    rows, width = outs[0].shape

    @pl.when(step == 0)
    def _():
        for spot, block in enumerate(blocks):
            rows_ref[spot * rows : (spot + 1) * rows, :] = block[:, :width]

    gate_value = jnp.dot(rows_ref[...], gate_ref[0], preferred_element_type=jnp.float32)
    upward = jnp.dot(rows_ref[...], up_ref[0], preferred_element_type=jnp.float32)
    hidden = (gate_value / (1.0 + jnp.exp(-gate_value)) * upward).astype(jnp.bfloat16)
    part = jnp.dot(hidden, down_ref[0], preferred_element_type=jnp.float32)

    @pl.when(step == 0)
    def _():
        total_ref[...] = part

    @pl.when(step > 0)
    def _():
        total_ref[...] += part

    @pl.when(step == steps - 1)
    def _():
        for spot, (block, out) in enumerate(zip(blocks, outs)):
            units = block[:, width:].astype(jnp.float32)
            lane = lax.broadcasted_iota(jnp.int32, units.shape, 1)
            own = jnp.sum(jnp.where(lane == own_ref[0], units, 0.0), axis=1, keepdims=True)
            weight = own / jnp.sum(units, axis=1, keepdims=True)
            expert_out = total_ref[spot * rows : (spot + 1) * rows, :].astype(jnp.bfloat16)
            out[...] = (weight * expert_out.astype(jnp.float32)).astype(jnp.bfloat16)


def expert_rows(own, blocks, gate_matrix, up_matrix, down_matrix):
    rows, padded = blocks[0].shape
    width, hidden_width = gate_matrix.shape[1:]
    tile = 256
    block_spec = pl.BlockSpec((rows, padded), lambda i, own: (0, 0))
    column_spec = pl.BlockSpec((1, width, tile), lambda i, own: (0, 0, i))
    return pl.pallas_call(
        expert_kernel,
        grid_spec=pltpu.PrefetchScalarGridSpec(
            num_scalar_prefetch=1,
            grid=(hidden_width // tile,),
            in_specs=[block_spec] * PLANE
            + [column_spec, column_spec, pl.BlockSpec((1, tile, width), lambda i, own: (0, i, 0))],
            out_specs=[pl.BlockSpec((rows, width), lambda i, own: (0, 0))] * PLANE,
            scratch_shapes=[
                pltpu.VMEM((PLANE * rows, width), jnp.bfloat16),
                pltpu.VMEM((PLANE * rows, width), jnp.float32),
            ],
        ),
        out_shape=[jax.ShapeDtypeStruct((rows, width), jnp.bfloat16)] * PLANE,
        compiler_params=pltpu.CompilerParams(vmem_limit_bytes=32 * 1024 * 1024),
        cost_estimate=pl.CostEstimate(
            flops=6 * PLANE * rows * width * hidden_width,
            bytes_accessed=6 * width * hidden_width + 4 * PLANE * rows * padded,
            transcendentals=PLANE * rows * hidden_width,
        ),
    )(own, *blocks, gate_matrix, up_matrix, down_matrix)


def dense_plan(tokens, expert_ids, gate_units, gate_matrix, up_matrix, down_matrix):
    devices = lax.axis_size("expert")
    planes = devices // PLANE
    everyone = range(devices)
    core_pairs = [(i, i ^ 1) for i in everyone]
    side_pairs = [(i, i ^ 2) for i in everyone]

    def core(block):
        return lax.ppermute(block, "expert", core_pairs)

    def side(block):
        return lax.ppermute(block, "expert", side_pairs)

    def turn(block, planes_on):
        pairs = [(i, (i + planes_on * PLANE) % devices) for i in everyone]
        return lax.ppermute(block, "expert", pairs)

    lane = jnp.arange(LANES, dtype=jnp.int32)
    chosen = expert_ids[:, :, None] == lane[None, None, :]
    units = jnp.sum(jnp.where(chosen, gate_units[:, :, None], 0), axis=1)
    mine = jnp.concatenate([tokens, units.astype(jnp.bfloat16)], axis=1)
    own = lax.axis_index("expert").astype(jnp.int32).reshape(1)

    order = list(range(1, planes)) + [0]
    arrived = {on: mine if on == 0 else turn(mine, on) for on in order}
    total = []
    for on in order:
        here = arrived[on]
        beside = side(here)
        parts = expert_rows(
            own, [here, beside, core(here), core(beside)], gate_matrix, up_matrix, down_matrix
        )
        parts = list(parts)
        away = core(parts[3]).astype(jnp.float32) + parts[1].astype(jnp.float32)
        away = side(away.astype(jnp.bfloat16)).astype(jnp.float32)
        near = core(parts[2]).astype(jnp.float32) + parts[0].astype(jnp.float32)
        plane_sum = (near + away).astype(jnp.bfloat16)
        total.append(plane_sum if on == 0 else turn(plane_sum, planes - on))
    mixed = functools.reduce(lambda a, b: a + b, [t.astype(jnp.float32) for t in total])
    return mixed.astype(jnp.bfloat16)


def per_device(tokens, expert_ids, gate_units, gate_matrix, up_matrix, down_matrix):
    devices = lax.axis_size("expert")
    tok_rows, top_count = expert_ids.shape
    dense = 2 * tok_rows * top_count // devices >= tok_rows
    if dense and devices % PLANE == 0 and devices <= LANES:
        plan = dense_plan
    else:
        plan = routed_plan
    return plan(tokens, expert_ids, gate_units, gate_matrix, up_matrix, down_matrix)


def solution(mesh):
    placed = (
        P(("groups", "expert"), None),
        P(("groups", "expert"), None),
        P(("groups", "expert"), None),
        P("expert", None, None),
        P("expert", None, None),
        P("expert", None, None),
    )
    return jax.shard_map(
        per_device,
        mesh=mesh,
        in_specs=placed,
        out_specs=P(("groups", "expert"), None),
        check_vma=False,
    )
```

```python
import functools

import jax
import jax.numpy as jnp
from jax import lax
from jax.experimental import pallas as pl
from jax.experimental.pallas import tpu as pltpu
from jax.sharding import PartitionSpec as P

LANES = 128
PLANE = 4


def swiglu_rows(rows_in, gate_w, up_w, down_w):
    gate_value = jnp.dot(rows_in, gate_w, preferred_element_type=jnp.float32)
    upward = jnp.dot(rows_in, up_w, preferred_element_type=jnp.float32)
    hidden = (jax.nn.silu(gate_value) * upward).astype(jnp.bfloat16)
    return jnp.dot(hidden, down_w, preferred_element_type=jnp.float32).astype(jnp.bfloat16)


def routed_plan(tokens, expert_ids, gate_units, gate_matrix, up_matrix, down_matrix):
    devices = lax.axis_size("expert")
    tok_rows, top_count = expert_ids.shape
    feature_width = tokens.shape[1]
    route_rows = tok_rows * top_count
    capacity = 2 * route_rows // devices
    flat_ids = expert_ids.reshape(route_rows)
    expert_range = jnp.arange(devices, dtype=jnp.int32)
    onehot = (flat_ids[:, None] == expert_range[None, :]).astype(jnp.int32)
    earlier = jnp.cumsum(onehot, axis=0) - onehot
    position = jnp.sum(earlier * onehot, axis=1)
    routed = jnp.repeat(tokens, top_count, axis=0)
    gate_scale = gate_units.astype(jnp.float32)
    weight = gate_scale / jnp.sum(gate_scale, axis=1, keepdims=True)
    flat_slot = flat_ids * capacity + position
    outgoing = (
        jnp.zeros((devices * capacity, feature_width), jnp.bfloat16).at[flat_slot].set(routed)
    )
    received = lax.all_to_all(
        outgoing.reshape(devices, capacity, feature_width),
        "expert",
        split_axis=0,
        concat_axis=0,
        tiled=True,
    )
    result = swiglu_rows(
        received.reshape(-1, feature_width), gate_matrix[0], up_matrix[0], down_matrix[0]
    )
    back_buffer = lax.all_to_all(
        result.reshape(received.shape), "expert", split_axis=0, concat_axis=0, tiled=True
    )
    returned = back_buffer.reshape(-1, feature_width)[flat_slot]
    expert_out = returned.reshape(tok_rows, top_count, feature_width).astype(jnp.float32)
    mixed = jnp.einsum("tk,tkd->td", weight, expert_out)
    return mixed.astype(jnp.bfloat16)


def pack_kernel(tokens_hbm, ids_hbm, units_hbm, out_ref, ids_ref, units_ref, sems):
    top_count, rows = ids_ref.shape
    width = tokens_hbm.shape[1]
    copies = [
        pltpu.make_async_copy(tokens_hbm, out_ref.at[:, :width], sems.at[0]),
        pltpu.make_async_copy(ids_hbm, ids_ref, sems.at[1]),
        pltpu.make_async_copy(units_hbm, units_ref, sems.at[2]),
    ]
    for copy in copies:
        copy.start()
    copies[1].wait()
    copies[2].wait()
    expert = lax.broadcasted_iota(jnp.int32, (LANES, rows), 0)
    units = jnp.zeros((LANES, rows), jnp.int32)
    for k in range(top_count):
        units += jnp.where(expert == ids_ref[k : k + 1, :], units_ref[k : k + 1, :], 0)
    out_ref[:, width:] = units.astype(jnp.float32).T.astype(jnp.bfloat16)
    copies[0].wait()


def pack(tokens, expert_ids, gate_units):
    rows, width = tokens.shape
    routes = (expert_ids.shape[1], rows)
    return pl.pallas_call(
        pack_kernel,
        in_specs=[pl.BlockSpec(memory_space=pltpu.HBM)] * 3,
        out_specs=pl.BlockSpec(memory_space=pltpu.VMEM),
        out_shape=jax.ShapeDtypeStruct((rows, width + LANES), tokens.dtype),
        scratch_shapes=[
            pltpu.VMEM(routes, jnp.int32),
            pltpu.VMEM(routes, jnp.int32),
            pltpu.SemaphoreType.DMA((3,)),
        ],
        compiler_params=pltpu.CompilerParams(vmem_limit_bytes=60 * 1024 * 1024),
        cost_estimate=pl.CostEstimate(flops=0, bytes_accessed=4 * rows * width, transcendentals=0),
    )(tokens, expert_ids.T, gate_units.T)


def load_kernel(*refs):
    count = len(refs) // 2
    sources, (targets, sems) = refs[:count], (refs[count : 2 * count], refs[2 * count])
    copies = [
        pltpu.make_async_copy(source, target, sems.at[spot])
        for spot, (source, target) in enumerate(zip(sources, targets))
    ]
    for copy in copies:
        copy.start()
    for copy in copies:
        copy.wait()


def load(*matrices):
    return pl.pallas_call(
        load_kernel,
        in_specs=[pl.BlockSpec(memory_space=pltpu.HBM)] * len(matrices),
        out_specs=[pl.BlockSpec(memory_space=pltpu.VMEM)] * len(matrices),
        out_shape=[pltpu.VMEM(m.shape, m.dtype) for m in matrices],
        scratch_shapes=[pltpu.SemaphoreType.DMA((len(matrices),))],
        compiler_params=pltpu.CompilerParams(vmem_limit_bytes=44 * 1024 * 1024),
        cost_estimate=pl.CostEstimate(
            flops=0, bytes_accessed=sum(2 * m.size for m in matrices), transcendentals=0
        ),
    )(*matrices)


def expert_kernel(own_ref, *refs):
    blocks, (gate_ref, up_ref, down_ref) = refs[:PLANE], refs[PLANE : PLANE + 3]
    outs, total_ref = refs[PLANE + 3 : PLANE + 5], refs[PLANE + 5]
    rows, (width, hidden_width) = blocks[0].shape[0], gate_ref.shape[1:]
    tile = 256
    tokens = jnp.concatenate([block[:, :width] for block in blocks], axis=0)
    for start in range(0, hidden_width, tile):
        columns = slice(start, start + tile)
        gate_value = jnp.dot(tokens, gate_ref[0, :, columns], preferred_element_type=jnp.float32)
        upward = jnp.dot(tokens, up_ref[0, :, columns], preferred_element_type=jnp.float32)
        hidden = (gate_value / (1.0 + jnp.exp(-gate_value)) * upward).astype(jnp.bfloat16)
        part = jnp.dot(hidden, down_ref[0, columns, :], preferred_element_type=jnp.float32)
        if start == 0:
            total_ref[...] = part
        else:
            total_ref[...] += part
    for spot, block in enumerate(blocks):
        units = block[:, width:].astype(jnp.float32)
        lane = lax.broadcasted_iota(jnp.int32, units.shape, 1)
        own = jnp.sum(jnp.where(lane == own_ref[0], units, 0.0), axis=1, keepdims=True)
        weight = own / jnp.sum(units, axis=1, keepdims=True)
        expert_out = total_ref[spot * rows : (spot + 1) * rows, :].astype(jnp.bfloat16)
        half = slice(spot % 2 * rows, (spot % 2 + 1) * rows)
        outs[spot // 2][half, :] = (weight * expert_out.astype(jnp.float32)).astype(jnp.bfloat16)


def expert_rows(own, blocks, gate_matrix, up_matrix, down_matrix):
    rows, padded = blocks[0].shape
    width, hidden_width = gate_matrix.shape[1:]
    in_vmem = pl.BlockSpec(memory_space=pltpu.VMEM)
    return pl.pallas_call(
        expert_kernel,
        in_specs=[pl.BlockSpec(memory_space=pltpu.SMEM)] + [in_vmem] * (PLANE + 3),
        out_specs=[in_vmem] * 2,
        out_shape=[jax.ShapeDtypeStruct((2 * rows, width), jnp.bfloat16)] * 2,
        scratch_shapes=[pltpu.VMEM((PLANE * rows, width), jnp.float32)],
        compiler_params=pltpu.CompilerParams(vmem_limit_bytes=16 * 1024 * 1024),
        cost_estimate=pl.CostEstimate(
            flops=6 * PLANE * rows * width * hidden_width,
            bytes_accessed=4 * PLANE * rows * padded,
            transcendentals=PLANE * rows * hidden_width,
        ),
    )(own, *blocks, gate_matrix, up_matrix, down_matrix)


def dense_plan(tokens, expert_ids, gate_units, gate_matrix, up_matrix, down_matrix):
    devices = lax.axis_size("expert")
    planes = devices // PLANE
    everyone = range(devices)
    core_pairs = [(i, i ^ 1) for i in everyone]
    side_pairs = [(i, i ^ 2) for i in everyone]

    def core(block):
        return lax.ppermute(block, "expert", core_pairs)

    def side(block):
        return lax.ppermute(block, "expert", side_pairs)

    def turn(block, planes_on):
        pairs = [(i, (i + planes_on * PLANE) % devices) for i in everyone]
        return lax.ppermute(block, "expert", pairs)

    own = lax.axis_index("expert").astype(jnp.int32).reshape(1)
    mine = pack(tokens, expert_ids, gate_units)
    rows = tokens.shape[0]

    def after(block, *earlier):
        return lax.optimization_barrier((block, *earlier))[0]

    here, beside, core_here, core_beside = {0: mine}, {}, {}, {}
    keep, give, near, away, sums = {}, {}, {}, {}, {}

    def experts(on, *earlier):
        four = [beside[on], here[on], core_beside[on], core_here[on]]
        keep[on], give[on] = expert_rows(after(own, *earlier), four, *weights)
        return give[on]

    def wide(block):
        return block.astype(jnp.float32)

    def back(on, *earlier):
        got = core(after(give[on], *earlier))
        away[on] = (wide(keep[on][:rows]) + wide(got[:rows])).astype(jnp.bfloat16)
        near[on] = wide(keep[on][rows:]) + wide(got[rows:])
        return away[on]

    def across(on, *earlier):
        moved = side(after(away[on], *earlier))
        sums[on] = (near[on] + wide(moved)).astype(jnp.bfloat16)
        return sums[on]

    def home(on, *earlier):
        sums[on] = turn(after(sums[on], *earlier), planes - on)

    here[1] = turn(mine, 1)
    here[3] = turn(mine, 3)
    beside[0] = side(mine)
    core_here[0] = core(mine)
    core_beside[0] = core(beside[0])
    beside[1] = side(after(here[1], beside[0]))
    here[2] = turn(here[1], 1)
    core_here[1] = core(here[1])
    beside[3] = side(after(here[3], here[1]))
    core_here[3] = core(after(here[3], here[1]))
    core_beside[1] = core(after(beside[1], here[3]))
    beside[2] = side(after(here[2], beside[1]))
    core_here[2] = core(after(here[2], beside[1]))
    weights = load(
        *lax.optimization_barrier((gate_matrix, up_matrix, down_matrix, here[2]))[:3]
    )
    experts(1)
    back(1)
    core_beside[3] = core(beside[3])
    across(1)
    experts(3, give[1])
    back(3)
    across(3, away[1])
    core_beside[2] = core(beside[2])
    experts(2, away[3])
    back(2)
    experts(0, sums[1], give[2])
    back(0, give[2])
    home(1)
    across(2)
    home(3)
    across(0, away[2])
    home(2)
    mixed = functools.reduce(lambda a, b: a + b, [wide(sums[on]) for on in range(4)])
    return mixed.astype(jnp.bfloat16)


def per_device(tokens, expert_ids, gate_units, gate_matrix, up_matrix, down_matrix):
    devices = lax.axis_size("expert")
    tok_rows, top_count = expert_ids.shape
    dense = 2 * tok_rows * top_count // devices >= tok_rows
    if dense and devices % PLANE == 0 and devices <= LANES:
        plan = dense_plan
    else:
        plan = routed_plan
    return plan(tokens, expert_ids, gate_units, gate_matrix, up_matrix, down_matrix)


def solution(mesh):
    placed = (
        P(("groups", "expert"), None),
        P(("groups", "expert"), None),
        P(("groups", "expert"), None),
        P("expert", None, None),
        P("expert", None, None),
        P("expert", None, None),
    )
    return jax.shard_map(
        per_device,
        mesh=mesh,
        in_specs=placed,
        out_specs=P(("groups", "expert"), None),
        check_vma=False,
    )
```

```python
import functools

import jax
import jax.numpy as jnp
from jax import lax
from jax.experimental import pallas as pl
from jax.experimental.pallas import tpu as pltpu
from jax.sharding import PartitionSpec as P

LANES = 128
PLANE = 4
PLANES = 4
ORDER = (
    ("x", 0, 0), ("z", 1, 1), ("z", 3, 1), ("x", 1, 1), ("z", 2, 1),
    ("w", 0, 1), ("k", 1, 0), ("x", 3, 1), ("k", 3, 1), ("k", 0, 1),
    ("x", 2, 1), ("c", 1, 0), ("k", 2, 1), ("c", 2, 0), ("c", 3, 1),
    ("s", 1, 2), ("s", 2, 0), ("c", 0, 1), ("s", 3, 0), ("s", 0, 0),
)


def swiglu_rows(rows_in, gate_w, up_w, down_w):
    gate_value = jnp.dot(rows_in, gate_w, preferred_element_type=jnp.float32)
    upward = jnp.dot(rows_in, up_w, preferred_element_type=jnp.float32)
    hidden = (jax.nn.silu(gate_value) * upward).astype(jnp.bfloat16)
    return jnp.dot(hidden, down_w, preferred_element_type=jnp.float32).astype(jnp.bfloat16)


def routed_plan(tokens, expert_ids, gate_units, gate_matrix, up_matrix, down_matrix):
    devices = lax.axis_size("expert")
    tok_rows, top_count = expert_ids.shape
    feature_width = tokens.shape[1]
    route_rows = tok_rows * top_count
    capacity = 2 * route_rows // devices
    flat_ids = expert_ids.reshape(route_rows)
    expert_range = jnp.arange(devices, dtype=jnp.int32)
    onehot = (flat_ids[:, None] == expert_range[None, :]).astype(jnp.int32)
    earlier = jnp.cumsum(onehot, axis=0) - onehot
    position = jnp.sum(earlier * onehot, axis=1)
    routed = jnp.repeat(tokens, top_count, axis=0)
    gate_scale = gate_units.astype(jnp.float32)
    weight = gate_scale / jnp.sum(gate_scale, axis=1, keepdims=True)
    flat_slot = flat_ids * capacity + position
    outgoing = (
        jnp.zeros((devices * capacity, feature_width), jnp.bfloat16).at[flat_slot].set(routed)
    )
    received = lax.all_to_all(
        outgoing.reshape(devices, capacity, feature_width),
        "expert",
        split_axis=0,
        concat_axis=0,
        tiled=True,
    )
    result = swiglu_rows(
        received.reshape(-1, feature_width), gate_matrix[0], up_matrix[0], down_matrix[0]
    )
    back_buffer = lax.all_to_all(
        result.reshape(received.shape), "expert", split_axis=0, concat_axis=0, tiled=True
    )
    returned = back_buffer.reshape(-1, feature_width)[flat_slot]
    expert_out = returned.reshape(tok_rows, top_count, feature_width).astype(jnp.float32)
    mixed = jnp.einsum("tk,tkd->td", weight, expert_out)
    return mixed.astype(jnp.bfloat16)


def pack_kernel(tokens_hbm, ids_hbm, units_hbm, out_ref, ids_ref, units_ref, sems):
    top_count, rows = ids_ref.shape
    width = tokens_hbm.shape[1]
    copies = [
        pltpu.make_async_copy(tokens_hbm, out_ref.at[:, :width], sems.at[0]),
        pltpu.make_async_copy(ids_hbm, ids_ref, sems.at[1]),
        pltpu.make_async_copy(units_hbm, units_ref, sems.at[2]),
    ]
    for copy in copies:
        copy.start()
    copies[1].wait()
    copies[2].wait()
    expert = lax.broadcasted_iota(jnp.int32, (LANES, rows), 0)
    units = jnp.zeros((LANES, rows), jnp.int32)
    for k in range(top_count):
        units += jnp.where(expert == ids_ref[k : k + 1, :], units_ref[k : k + 1, :], 0)
    out_ref[:, width:] = units.astype(jnp.float32).T.astype(jnp.bfloat16)
    copies[0].wait()


def pack(tokens, expert_ids, gate_units):
    rows, width = tokens.shape
    routes = (expert_ids.shape[1], rows)
    return pl.pallas_call(
        pack_kernel,
        in_specs=[pl.BlockSpec(memory_space=pltpu.HBM)] * 3,
        out_specs=pl.BlockSpec(memory_space=pltpu.VMEM),
        out_shape=jax.ShapeDtypeStruct((rows, width + LANES), tokens.dtype),
        scratch_shapes=[
            pltpu.VMEM(routes, jnp.int32),
            pltpu.VMEM(routes, jnp.int32),
            pltpu.SemaphoreType.DMA((3,)),
        ],
        compiler_params=pltpu.CompilerParams(vmem_limit_bytes=60 * 1024 * 1024),
        cost_estimate=pl.CostEstimate(flops=0, bytes_accessed=4 * rows * width, transcendentals=0),
    )(tokens, expert_ids.T, gate_units.T)


def load_kernel(*refs):
    count = len(refs) // 2
    sources, (targets, sems) = refs[:count], (refs[count : 2 * count], refs[2 * count])
    copies = [
        pltpu.make_async_copy(source, target, sems.at[spot])
        for spot, (source, target) in enumerate(zip(sources, targets))
    ]
    for copy in copies:
        copy.start()
    for copy in copies:
        copy.wait()


def load(*matrices):
    return pl.pallas_call(
        load_kernel,
        in_specs=[pl.BlockSpec(memory_space=pltpu.HBM)] * len(matrices),
        out_specs=[pl.BlockSpec(memory_space=pltpu.VMEM)] * len(matrices),
        out_shape=[pltpu.VMEM(m.shape, m.dtype) for m in matrices],
        scratch_shapes=[pltpu.SemaphoreType.DMA((len(matrices),))],
        compiler_params=pltpu.CompilerParams(vmem_limit_bytes=44 * 1024 * 1024),
        cost_estimate=pl.CostEstimate(flops=0, bytes_accessed=0, transcendentals=0),
    )(*matrices)


def expert_kernel(own_ref, *refs):
    blocks, (gate_ref, up_ref, down_ref) = refs[:PLANE], refs[PLANE : PLANE + 3]
    outs, total_ref = refs[PLANE + 3 : PLANE + 5], refs[PLANE + 5]
    rows, (width, hidden_width) = blocks[0].shape[0], gate_ref.shape[1:]
    tile = 256
    tokens = jnp.concatenate([block[:, :width] for block in blocks], axis=0)
    for start in range(0, hidden_width, tile):
        columns = slice(start, start + tile)
        gate_value = jnp.dot(tokens, gate_ref[0, :, columns], preferred_element_type=jnp.float32)
        upward = jnp.dot(tokens, up_ref[0, :, columns], preferred_element_type=jnp.float32)
        hidden = (gate_value / (1.0 + jnp.exp(-gate_value)) * upward).astype(jnp.bfloat16)
        part = jnp.dot(hidden, down_ref[0, columns, :], preferred_element_type=jnp.float32)
        if start == 0:
            total_ref[...] = part
        else:
            total_ref[...] += part
    for spot, block in enumerate(blocks):
        units = block[:, width:].astype(jnp.float32)
        lane = lax.broadcasted_iota(jnp.int32, units.shape, 1)
        own = jnp.sum(jnp.where(lane == own_ref[0], units, 0.0), axis=1, keepdims=True)
        weight = own / jnp.sum(units, axis=1, keepdims=True)
        expert_out = total_ref[spot * rows : (spot + 1) * rows, :].astype(jnp.bfloat16)
        half = slice(spot % 2 * rows, (spot % 2 + 1) * rows)
        outs[spot // 2][half, :] = (weight * expert_out.astype(jnp.float32)).astype(jnp.bfloat16)


def expert_rows(own, blocks, gate_matrix, up_matrix, down_matrix):
    rows, padded = blocks[0].shape
    width, hidden_width = gate_matrix.shape[1:]
    in_vmem = pl.BlockSpec(memory_space=pltpu.VMEM)
    return pl.pallas_call(
        expert_kernel,
        in_specs=[pl.BlockSpec(memory_space=pltpu.SMEM)] + [in_vmem] * (PLANE + 3),
        out_specs=[in_vmem] * 2,
        out_shape=[jax.ShapeDtypeStruct((2 * rows, width), jnp.bfloat16)] * 2,
        scratch_shapes=[pltpu.VMEM((PLANE * rows, width), jnp.float32)],
        compiler_params=pltpu.CompilerParams(vmem_limit_bytes=16 * 1024 * 1024),
        cost_estimate=pl.CostEstimate(flops=0, bytes_accessed=0, transcendentals=0),
    )(own, *blocks, gate_matrix, up_matrix, down_matrix)


def dense_plan(tokens, expert_ids, gate_units, *matrices):
    devices = lax.axis_size("expert")
    planes = PLANES
    everyone = range(devices)
    core_pairs = [(i, i ^ 1) for i in everyone]
    side_pairs = [(i, i ^ 2) for i in everyone]

    def core(block):
        return lax.ppermute(block, "expert", core_pairs)

    def side(block):
        return lax.ppermute(block, "expert", side_pairs)

    def turn(block, planes_on):
        pairs = [(i, (i + planes_on * PLANE) % devices) for i in everyone]
        return lax.ppermute(block, "expert", pairs)

    own = lax.axis_index("expert").astype(jnp.int32).reshape(1)
    mine = pack(tokens, expert_ids, gate_units)
    rows = tokens.shape[0]

    here, beside, core_here, core_beside, weights = {0: mine}, {}, {}, {}, []
    keep, give, moved, near, away, sums, homes = {}, {}, {}, {}, {}, {}, []
    done = []

    def wide(block):
        return block.astype(jnp.float32)

    def after(block):
        earlier = done[max(0, len(done) - back) :]
        return lax.optimization_barrier((block, *earlier))[0]

    for what, on, back in ORDER:
        if what == "z":
            here[on] = turn(here[1], 1) if on == 2 else turn(mine, on)
            beside[on] = side(after(here[on]))
            core_here[on] = core(after(here[on]))
            done.append(here[on])
        elif what == "x":
            if on == 0:
                beside[0], core_here[0] = side(mine), core(mine)
            core_beside[on] = core(after(beside[on]))
            done.append(beside[on])
        elif what == "k":
            blocks = [beside[on], here[on], core_beside[on], core_here[on]]
            keep[on], give[on] = expert_rows(after(own), blocks, *weights)
            done.append(give[on])
        elif what == "w":
            weights = load(*(after(matrix) for matrix in matrices))
        elif what == "c":
            got = core(give[on])
            near[on] = wide(keep[on][rows:]) + wide(got[rows:])
            away[on] = (wide(keep[on][:rows]) + wide(got[:rows])).astype(jnp.bfloat16)
            moved[on] = side(after(away[on]))
            done.append(away[on])
        else:
            sums[on] = (near[on] + wide(moved[on])).astype(jnp.bfloat16)
            homes.append(turn(after(sums[on]), planes - on) if on else sums[on])
            done.append(sums[on])
    mixed = functools.reduce(lambda a, b: a + b, [wide(home) for home in homes])
    return mixed.astype(jnp.bfloat16)


def per_device(tokens, expert_ids, gate_units, gate_matrix, up_matrix, down_matrix):
    devices = lax.axis_size("expert")
    tok_rows, top_count = expert_ids.shape
    dense = 2 * tok_rows * top_count // devices >= tok_rows
    if dense and devices == PLANE * PLANES:
        plan = dense_plan
    else:
        plan = routed_plan
    return plan(tokens, expert_ids, gate_units, gate_matrix, up_matrix, down_matrix)


def solution(mesh):
    placed = (
        P(("groups", "expert"), None),
        P(("groups", "expert"), None),
        P(("groups", "expert"), None),
        P("expert", None, None),
        P("expert", None, None),
        P("expert", None, None),
    )
    return jax.shard_map(
        per_device,
        mesh=mesh,
        in_specs=placed,
        out_specs=P(("groups", "expert"), None),
        check_vma=False,
    )
```

```python
import functools

import jax
import jax.numpy as jnp
from jax import lax
from jax.experimental import pallas as pl
from jax.experimental.pallas import tpu as pltpu
from jax.sharding import PartitionSpec as P

LANES = 128
PLANE = 4
PLANES = 4
ORDER = (
    ("x", 0, 0), ("z", 1, 1), ("z", 3, 1), ("x", 1, 1), ("z", 2, 1),
    ("w", 0, 1), ("k", 1, 0), ("x", 3, 1), ("k", 0, 1), ("k", 3, 1),
    ("x", 2, 1), ("c", 1, 0), ("k", 2, 1), ("c", 2, 0), ("c", 3, 1),
    ("s", 1, 2), ("s", 2, 0), ("c", 0, 1), ("s", 3, 0), ("s", 0, 0),
)


def swiglu_rows(rows_in, gate_w, up_w, down_w):
    gate_value = jnp.dot(rows_in, gate_w, preferred_element_type=jnp.float32)
    upward = jnp.dot(rows_in, up_w, preferred_element_type=jnp.float32)
    hidden = (jax.nn.silu(gate_value) * upward).astype(jnp.bfloat16)
    return jnp.dot(hidden, down_w, preferred_element_type=jnp.float32).astype(jnp.bfloat16)


def routed_plan(tokens, expert_ids, gate_units, gate_matrix, up_matrix, down_matrix):
    devices = lax.axis_size("expert")
    tok_rows, top_count = expert_ids.shape
    feature_width = tokens.shape[1]
    route_rows = tok_rows * top_count
    capacity = 2 * route_rows // devices
    flat_ids = expert_ids.reshape(route_rows)
    expert_range = jnp.arange(devices, dtype=jnp.int32)
    onehot = (flat_ids[:, None] == expert_range[None, :]).astype(jnp.int32)
    earlier = jnp.cumsum(onehot, axis=0) - onehot
    position = jnp.sum(earlier * onehot, axis=1)
    routed = jnp.repeat(tokens, top_count, axis=0)
    gate_scale = gate_units.astype(jnp.float32)
    weight = gate_scale / jnp.sum(gate_scale, axis=1, keepdims=True)
    flat_slot = flat_ids * capacity + position
    outgoing = (
        jnp.zeros((devices * capacity, feature_width), jnp.bfloat16).at[flat_slot].set(routed)
    )
    received = lax.all_to_all(
        outgoing.reshape(devices, capacity, feature_width),
        "expert",
        split_axis=0,
        concat_axis=0,
        tiled=True,
    )
    result = swiglu_rows(
        received.reshape(-1, feature_width), gate_matrix[0], up_matrix[0], down_matrix[0]
    )
    back_buffer = lax.all_to_all(
        result.reshape(received.shape), "expert", split_axis=0, concat_axis=0, tiled=True
    )
    returned = back_buffer.reshape(-1, feature_width)[flat_slot]
    expert_out = returned.reshape(tok_rows, top_count, feature_width).astype(jnp.float32)
    mixed = jnp.einsum("tk,tkd->td", weight, expert_out)
    return mixed.astype(jnp.bfloat16)


def pack_kernel(tokens_hbm, ids_hbm, units_hbm, out_ref, ids_ref, units_ref, sems):
    top_count, rows = ids_ref.shape
    width = tokens_hbm.shape[1]
    copies = [
        pltpu.make_async_copy(tokens_hbm, out_ref.at[:, :width], sems.at[0]),
        pltpu.make_async_copy(ids_hbm, ids_ref, sems.at[1]),
        pltpu.make_async_copy(units_hbm, units_ref, sems.at[2]),
    ]
    for copy in copies:
        copy.start()
    copies[1].wait()
    copies[2].wait()
    expert = lax.broadcasted_iota(jnp.int32, (LANES, rows), 0)
    units = jnp.zeros((LANES, rows), jnp.int32)
    for k in range(top_count):
        units += jnp.where(expert == ids_ref[k : k + 1, :], units_ref[k : k + 1, :], 0)
    out_ref[:, width:] = units.astype(jnp.float32).T.astype(jnp.bfloat16)
    copies[0].wait()


def pack(tokens, expert_ids, gate_units):
    rows, width = tokens.shape
    routes = (expert_ids.shape[1], rows)
    return pl.pallas_call(
        pack_kernel,
        in_specs=[pl.BlockSpec(memory_space=pltpu.HBM)] * 3,
        out_specs=pl.BlockSpec(memory_space=pltpu.VMEM),
        out_shape=jax.ShapeDtypeStruct((rows, width + LANES), tokens.dtype),
        scratch_shapes=[
            pltpu.VMEM(routes, jnp.int32),
            pltpu.VMEM(routes, jnp.int32),
            pltpu.SemaphoreType.DMA((3,)),
        ],
        compiler_params=pltpu.CompilerParams(vmem_limit_bytes=60 * 1024 * 1024),
        cost_estimate=pl.CostEstimate(flops=0, bytes_accessed=4 * rows * width, transcendentals=0),
    )(tokens, expert_ids.T, gate_units.T)


def load_kernel(*refs):
    count = len(refs) // 2
    sources, (targets, sems) = refs[:count], (refs[count : 2 * count], refs[2 * count])
    copies = [
        pltpu.make_async_copy(source, target, sems.at[spot])
        for spot, (source, target) in enumerate(zip(sources, targets))
    ]
    for copy in copies:
        copy.start()
    for copy in copies:
        copy.wait()


def load(*matrices):
    return pl.pallas_call(
        load_kernel,
        in_specs=[pl.BlockSpec(memory_space=pltpu.HBM)] * len(matrices),
        out_specs=[pl.BlockSpec(memory_space=pltpu.VMEM)] * len(matrices),
        out_shape=[pltpu.VMEM(m.shape, m.dtype) for m in matrices],
        scratch_shapes=[pltpu.SemaphoreType.DMA((len(matrices),))],
        compiler_params=pltpu.CompilerParams(vmem_limit_bytes=44 * 1024 * 1024),
        cost_estimate=pl.CostEstimate(flops=0, bytes_accessed=0, transcendentals=0),
    )(*matrices)


def expert_kernel(own_ref, *refs):
    blocks, (gate_ref, up_ref, down_ref) = refs[:PLANE], refs[PLANE : PLANE + 3]
    outs, total_ref = refs[PLANE + 3 : PLANE + 5], refs[PLANE + 5]
    rows, (width, hidden_width) = blocks[0].shape[0], gate_ref.shape[1:]
    tile = 256
    tokens = jnp.concatenate([block[:, :width] for block in blocks], axis=0)
    for start in range(0, hidden_width, tile):
        columns = slice(start, start + tile)
        gate_value = jnp.dot(tokens, gate_ref[0, :, columns], preferred_element_type=jnp.float32)
        upward = jnp.dot(tokens, up_ref[0, :, columns], preferred_element_type=jnp.float32)
        hidden = (gate_value / (1.0 + jnp.exp(-gate_value)) * upward).astype(jnp.bfloat16)
        part = jnp.dot(hidden, down_ref[0, columns, :], preferred_element_type=jnp.float32)
        if start == 0:
            total_ref[...] = part
        else:
            total_ref[...] += part
    for spot, block in enumerate(blocks):
        units = block[:, width:].astype(jnp.float32)
        lane = lax.broadcasted_iota(jnp.int32, units.shape, 1)
        own = jnp.sum(jnp.where(lane == own_ref[0], units, 0.0), axis=1, keepdims=True)
        weight = own / jnp.sum(units, axis=1, keepdims=True)
        expert_out = total_ref[spot * rows : (spot + 1) * rows, :].astype(jnp.bfloat16)
        half = slice(spot % 2 * rows, (spot % 2 + 1) * rows)
        outs[spot // 2][half, :] = (weight * expert_out.astype(jnp.float32)).astype(jnp.bfloat16)


def expert_rows(own, blocks, gate_matrix, up_matrix, down_matrix):
    rows, padded = blocks[0].shape
    width, hidden_width = gate_matrix.shape[1:]
    in_vmem = pl.BlockSpec(memory_space=pltpu.VMEM)
    return pl.pallas_call(
        expert_kernel,
        in_specs=[pl.BlockSpec(memory_space=pltpu.SMEM)] + [in_vmem] * (PLANE + 3),
        out_specs=[in_vmem] * 2,
        out_shape=[jax.ShapeDtypeStruct((2 * rows, width), jnp.bfloat16)] * 2,
        scratch_shapes=[pltpu.VMEM((PLANE * rows, width), jnp.float32)],
        compiler_params=pltpu.CompilerParams(vmem_limit_bytes=16 * 1024 * 1024),
        cost_estimate=pl.CostEstimate(flops=0, bytes_accessed=0, transcendentals=0),
    )(own, *blocks, gate_matrix, up_matrix, down_matrix)


def dense_plan(tokens, expert_ids, gate_units, *matrices):
    devices = lax.axis_size("expert")
    planes = PLANES
    everyone = range(devices)
    core_pairs = [(i, i ^ 1) for i in everyone]
    side_pairs = [(i, i ^ 2) for i in everyone]

    def core(block):
        return lax.ppermute(block, "expert", core_pairs)

    def side(block):
        return lax.ppermute(block, "expert", side_pairs)

    def turn(block, planes_on):
        pairs = [(i, (i + planes_on * PLANE) % devices) for i in everyone]
        return lax.ppermute(block, "expert", pairs)

    own = lax.axis_index("expert").astype(jnp.int32).reshape(1)
    mine = pack(tokens, expert_ids, gate_units)
    rows = tokens.shape[0]

    here, beside, core_here, core_beside, weights = {0: mine}, {}, {}, {}, []
    keep, give, moved, near, away, sums, homes = {}, {}, {}, {}, {}, {}, []
    done = []

    def wide(block):
        return block.astype(jnp.float32)

    def after(block):
        earlier = done[max(0, len(done) - back) :]
        return lax.optimization_barrier((block, *earlier))[0]

    for what, on, back in ORDER:
        if what == "z":
            here[on] = turn(here[1], 1) if on == 2 else turn(mine, on)
            beside[on] = side(after(here[on]))
            core_here[on] = core(after(here[on]))
            done.append(here[on])
        elif what == "x":
            if on == 0:
                beside[0], core_here[0] = side(mine), core(mine)
            core_beside[on] = core(after(beside[on]))
            done.append(beside[on])
        elif what == "k":
            blocks = [beside[on], here[on], core_beside[on], core_here[on]]
            keep[on], give[on] = expert_rows(after(own), blocks, *weights)
            done.append(give[on])
        elif what == "w":
            weights = load(*(after(matrix) for matrix in matrices))
        elif what == "c":
            got = core(give[on])
            near[on] = wide(keep[on][rows:]) + wide(got[rows:])
            away[on] = (wide(keep[on][:rows]) + wide(got[:rows])).astype(jnp.bfloat16)
            moved[on] = side(after(away[on]))
            done.append(away[on])
        else:
            sums[on] = (near[on] + wide(moved[on])).astype(jnp.bfloat16)
            homes.append(turn(after(sums[on]), planes - on) if on else sums[on])
            done.append(sums[on])
    mixed = functools.reduce(lambda a, b: a + b, [wide(home) for home in homes])
    return mixed.astype(jnp.bfloat16)


def per_device(tokens, expert_ids, gate_units, gate_matrix, up_matrix, down_matrix):
    devices = lax.axis_size("expert")
    tok_rows, top_count = expert_ids.shape
    dense = 2 * tok_rows * top_count // devices >= tok_rows
    if dense and devices == PLANE * PLANES:
        plan = dense_plan
    else:
        plan = routed_plan
    return plan(tokens, expert_ids, gate_units, gate_matrix, up_matrix, down_matrix)


def solution(mesh):
    placed = (
        P(("groups", "expert"), None),
        P(("groups", "expert"), None),
        P(("groups", "expert"), None),
        P("expert", None, None),
        P("expert", None, None),
        P("expert", None, None),
    )
    return jax.shard_map(
        per_device,
        mesh=mesh,
        in_specs=placed,
        out_specs=P(("groups", "expert"), None),
        check_vma=False,
    )
```

```python
import functools

import jax
import jax.numpy as jnp
from jax import lax
from jax.experimental import pallas as pl
from jax.experimental.pallas import tpu as pltpu
from jax.sharding import PartitionSpec as P

LANES = 128
PLANE = 4
PLANES = 4
ORDER = (
    ("x", 0, 0), ("z", 1, 1), ("z", 3, 1), ("x", 1, 1), ("z", 2, 1),
    ("w", 0, 1), ("k", 1, 0), ("x", 3, 1), ("k", 0, 1), ("k", 3, 1),
    ("x", 2, 1), ("c", 1, 0), ("k", 2, 1), ("c", 2, 0), ("c", 3, 1),
    ("s", 1, 2), ("s", 2, 0), ("c", 0, 1), ("s", 3, 0), ("s", 0, 0),
)


def swiglu_rows(rows_in, gate_w, up_w, down_w):
    gate_value = jnp.dot(rows_in, gate_w, preferred_element_type=jnp.float32)
    upward = jnp.dot(rows_in, up_w, preferred_element_type=jnp.float32)
    hidden = (jax.nn.silu(gate_value) * upward).astype(jnp.bfloat16)
    return jnp.dot(hidden, down_w, preferred_element_type=jnp.float32).astype(jnp.bfloat16)


def routed_plan(tokens, expert_ids, gate_units, gate_matrix, up_matrix, down_matrix):
    devices = lax.axis_size("expert")
    tok_rows, top_count = expert_ids.shape
    feature_width = tokens.shape[1]
    route_rows = tok_rows * top_count
    capacity = 2 * route_rows // devices
    flat_ids = expert_ids.reshape(route_rows)
    expert_range = jnp.arange(devices, dtype=jnp.int32)
    onehot = (flat_ids[:, None] == expert_range[None, :]).astype(jnp.int32)
    earlier = jnp.cumsum(onehot, axis=0) - onehot
    position = jnp.sum(earlier * onehot, axis=1)
    routed = jnp.repeat(tokens, top_count, axis=0)
    gate_scale = gate_units.astype(jnp.float32)
    weight = gate_scale / jnp.sum(gate_scale, axis=1, keepdims=True)
    flat_slot = flat_ids * capacity + position
    outgoing = (
        jnp.zeros((devices * capacity, feature_width), jnp.bfloat16).at[flat_slot].set(routed)
    )
    received = lax.all_to_all(
        outgoing.reshape(devices, capacity, feature_width),
        "expert",
        split_axis=0,
        concat_axis=0,
        tiled=True,
    )
    result = swiglu_rows(
        received.reshape(-1, feature_width), gate_matrix[0], up_matrix[0], down_matrix[0]
    )
    back_buffer = lax.all_to_all(
        result.reshape(received.shape), "expert", split_axis=0, concat_axis=0, tiled=True
    )
    returned = back_buffer.reshape(-1, feature_width)[flat_slot]
    expert_out = returned.reshape(tok_rows, top_count, feature_width).astype(jnp.float32)
    mixed = jnp.einsum("tk,tkd->td", weight, expert_out)
    return mixed.astype(jnp.bfloat16)


def pack_kernel(tokens_hbm, ids_hbm, units_hbm, out_ref, ids_ref, units_ref, sems):
    top_count, rows = ids_ref.shape
    width = tokens_hbm.shape[1]
    copies = [
        pltpu.make_async_copy(tokens_hbm, out_ref.at[:, :width], sems.at[0]),
        pltpu.make_async_copy(ids_hbm, ids_ref, sems.at[1]),
        pltpu.make_async_copy(units_hbm, units_ref, sems.at[2]),
    ]
    for copy in copies:
        copy.start()
    copies[1].wait()
    copies[2].wait()
    expert = lax.broadcasted_iota(jnp.int32, (LANES, rows), 0)
    units = jnp.zeros((LANES, rows), jnp.int32)
    for k in range(top_count):
        units += jnp.where(expert == ids_ref[k : k + 1, :], units_ref[k : k + 1, :], 0)
    out_ref[:, width:] = units.astype(jnp.float32).T.astype(jnp.bfloat16)
    copies[0].wait()


def pack(tokens, expert_ids, gate_units):
    rows, width = tokens.shape
    routes = (expert_ids.shape[1], rows)
    return pl.pallas_call(
        pack_kernel,
        in_specs=[pl.BlockSpec(memory_space=pltpu.HBM)] * 3,
        out_specs=pl.BlockSpec(memory_space=pltpu.VMEM),
        out_shape=jax.ShapeDtypeStruct((rows, width + LANES), tokens.dtype),
        scratch_shapes=[
            pltpu.VMEM(routes, jnp.int32),
            pltpu.VMEM(routes, jnp.int32),
            pltpu.SemaphoreType.DMA((3,)),
        ],
        compiler_params=pltpu.CompilerParams(vmem_limit_bytes=60 * 1024 * 1024),
        cost_estimate=pl.CostEstimate(flops=0, bytes_accessed=4 * rows * width, transcendentals=0),
    )(tokens, expert_ids.T, gate_units.T)


def load_kernel(*refs):
    count = len(refs) // 2
    sources, (targets, sems) = refs[:count], (refs[count : 2 * count], refs[2 * count])
    copies = [
        pltpu.make_async_copy(source, target, sems.at[spot])
        for spot, (source, target) in enumerate(zip(sources, targets))
    ]
    for copy in copies:
        copy.start()
    for copy in copies:
        copy.wait()


def load(*matrices):
    return pl.pallas_call(
        load_kernel,
        in_specs=[pl.BlockSpec(memory_space=pltpu.HBM)] * len(matrices),
        out_specs=[pl.BlockSpec(memory_space=pltpu.VMEM)] * len(matrices),
        out_shape=[pltpu.VMEM(m.shape, m.dtype) for m in matrices],
        scratch_shapes=[pltpu.SemaphoreType.DMA((len(matrices),))],
        compiler_params=pltpu.CompilerParams(vmem_limit_bytes=44 * 1024 * 1024),
        cost_estimate=pl.CostEstimate(flops=0, bytes_accessed=0, transcendentals=0),
    )(*matrices)


def expert_kernel(own_ref, *refs):
    blocks, (gate_ref, up_ref, down_ref) = refs[:PLANE], refs[PLANE : PLANE + 3]
    outs, total_ref = refs[PLANE + 3 : PLANE + 5], refs[PLANE + 5]
    rows, (width, hidden_width) = blocks[0].shape[0], gate_ref.shape[1:]
    tile = hidden_width
    tokens = jnp.concatenate([block[:, :width] for block in blocks], axis=0)
    for start in range(0, hidden_width, tile):
        columns = slice(start, start + tile)
        gate_value = jnp.dot(tokens, gate_ref[0, :, columns], preferred_element_type=jnp.float32)
        upward = jnp.dot(tokens, up_ref[0, :, columns], preferred_element_type=jnp.float32)
        hidden = (gate_value / (1.0 + jnp.exp(-gate_value)) * upward).astype(jnp.bfloat16)
        part = jnp.dot(hidden, down_ref[0, columns, :], preferred_element_type=jnp.float32)
        if start == 0:
            total_ref[...] = part
        else:
            total_ref[...] += part
    for spot, block in enumerate(blocks):
        units = block[:, width:].astype(jnp.float32)
        lane = lax.broadcasted_iota(jnp.int32, units.shape, 1)
        own = jnp.sum(jnp.where(lane == own_ref[0], units, 0.0), axis=1, keepdims=True)
        weight = own / jnp.sum(units, axis=1, keepdims=True)
        expert_out = total_ref[spot * rows : (spot + 1) * rows, :].astype(jnp.bfloat16)
        half = slice(spot % 2 * rows, (spot % 2 + 1) * rows)
        outs[spot // 2][half, :] = (weight * expert_out.astype(jnp.float32)).astype(jnp.bfloat16)


def expert_rows(own, blocks, gate_matrix, up_matrix, down_matrix):
    rows, padded = blocks[0].shape
    width, hidden_width = gate_matrix.shape[1:]
    in_vmem = pl.BlockSpec(memory_space=pltpu.VMEM)
    return pl.pallas_call(
        expert_kernel,
        in_specs=[pl.BlockSpec(memory_space=pltpu.SMEM)] + [in_vmem] * (PLANE + 3),
        out_specs=[in_vmem] * 2,
        out_shape=[jax.ShapeDtypeStruct((2 * rows, width), jnp.bfloat16)] * 2,
        scratch_shapes=[pltpu.VMEM((PLANE * rows, width), jnp.float32)],
        compiler_params=pltpu.CompilerParams(vmem_limit_bytes=16 * 1024 * 1024),
        cost_estimate=pl.CostEstimate(flops=0, bytes_accessed=0, transcendentals=0),
    )(own, *blocks, gate_matrix, up_matrix, down_matrix)


def dense_plan(tokens, expert_ids, gate_units, *matrices):
    devices = lax.axis_size("expert")
    planes = PLANES
    everyone = range(devices)
    core_pairs = [(i, i ^ 1) for i in everyone]
    side_pairs = [(i, i ^ 2) for i in everyone]

    def core(block):
        return lax.ppermute(block, "expert", core_pairs)

    def side(block):
        return lax.ppermute(block, "expert", side_pairs)

    def turn(block, planes_on):
        pairs = [(i, (i + planes_on * PLANE) % devices) for i in everyone]
        return lax.ppermute(block, "expert", pairs)

    own = lax.axis_index("expert").astype(jnp.int32).reshape(1)
    mine = pack(tokens, expert_ids, gate_units)
    rows = tokens.shape[0]

    here, beside, core_here, core_beside, weights = {0: mine}, {}, {}, {}, []
    keep, give, moved, near, away, sums, homes = {}, {}, {}, {}, {}, {}, []
    done = []

    def wide(block):
        return block.astype(jnp.float32)

    def after(block):
        earlier = done[max(0, len(done) - back) :]
        return lax.optimization_barrier((block, *earlier))[0]

    for what, on, back in ORDER:
        if what == "z":
            here[on] = turn(here[1], 1) if on == 2 else turn(mine, on)
            beside[on] = side(after(here[on]))
            core_here[on] = core(after(here[on]))
            done.append(here[on])
        elif what == "x":
            if on == 0:
                beside[0], core_here[0] = side(mine), core(mine)
            core_beside[on] = core(after(beside[on]))
            done.append(beside[on])
        elif what == "k":
            blocks = [beside[on], here[on], core_beside[on], core_here[on]]
            keep[on], give[on] = expert_rows(after(own), blocks, *weights)
            done.append(give[on])
        elif what == "w":
            weights = load(*(after(matrix) for matrix in matrices))
        elif what == "c":
            got = core(give[on])
            near[on] = wide(keep[on][rows:]) + wide(got[rows:])
            away[on] = (wide(keep[on][:rows]) + wide(got[:rows])).astype(jnp.bfloat16)
            moved[on] = side(after(away[on]))
            done.append(away[on])
        else:
            sums[on] = (near[on] + wide(moved[on])).astype(jnp.bfloat16)
            homes.append(turn(after(sums[on]), planes - on) if on else sums[on])
            done.append(sums[on])
    mixed = functools.reduce(lambda a, b: a + b, [wide(home) for home in homes])
    return mixed.astype(jnp.bfloat16)


def per_device(tokens, expert_ids, gate_units, gate_matrix, up_matrix, down_matrix):
    devices = lax.axis_size("expert")
    tok_rows, top_count = expert_ids.shape
    dense = 2 * tok_rows * top_count // devices >= tok_rows
    if dense and devices == PLANE * PLANES:
        plan = dense_plan
    else:
        plan = routed_plan
    return plan(tokens, expert_ids, gate_units, gate_matrix, up_matrix, down_matrix)


def solution(mesh):
    placed = (
        P(("groups", "expert"), None),
        P(("groups", "expert"), None),
        P(("groups", "expert"), None),
        P("expert", None, None),
        P("expert", None, None),
        P("expert", None, None),
    )
    return jax.shard_map(
        per_device,
        mesh=mesh,
        in_specs=placed,
        out_specs=P(("groups", "expert"), None),
        check_vma=False,
    )
```
